32 devices in a mesh: row: 4 (over x, core), col: 8 (over z, y).
Axes of the slice: x: 2, y: 2, z: 4, core: 2. Of those that a mesh axis runs over, the one named last changes fastest.
Arguments:
- matrix: float32 [8192, 4096], P('row', 'col'), may hold values from 0 to 2, as said below
Outputs:
- factored: float32 [8192, 4096], P('row', 'col')
The draws below stay inside these ranges and needn't reach their ends.
Inputs may be any that keep to these rules, and one draw needn't show every extreme that they name: In grid order, the matrix is the leading 4096 columns of a symmetric positive definite matrix of order 8192.
All inputs are finite; a program needn't handle non-finite values.
Results may differ from the reference program's by a relative error of at most 0.0011.
Values may be sent and summed in bfloat16 or wider, within the bound.
A program may use at most 64 MiB of HBM per device.

```python
import jax
import jax.numpy as jnp
from jax import lax

TILE = 256
TR = 8
TC = 2
PANELS = 3
N_ROW = 4
N_COL = 8


def draw_matrix(key, part):
    point_key = jax.random.fold_in(key, 11)
    total_rows = TR * TILE * N_ROW
    total_cols = TC * TILE * N_COL
    stored_row = jnp.arange(total_rows, dtype=jnp.int32)
    row_device = stored_row // (TR * TILE)
    row_rest = stored_row % (TR * TILE)
    grid_row = (row_rest // TILE * N_ROW + row_device) * TILE + row_rest % TILE
    stored_col = jnp.arange(total_cols, dtype=jnp.int32)
    col_device = stored_col // (TC * TILE)
    col_rest = stored_col % (TC * TILE)
    grid_col = (col_rest // TILE * N_COL + col_device) * TILE + col_rest % TILE
    extents = jnp.array([1.0, 1.0, 1.0], dtype=jnp.float32)
    coordinates = jax.random.uniform(point_key, (3, total_rows), jnp.float32, 0.0, 1.0) * extents[:, None]
    row_points = coordinates[:, grid_row]
    col_points = coordinates[:, grid_col]
    squared = jnp.zeros((total_rows, total_cols), jnp.float32)
    for axis_number in range(3):
        offset = row_points[axis_number][:, None] - col_points[axis_number][None, :]
        squared = squared + offset * offset
    distance = jnp.sqrt(squared)
    on_diagonal = grid_row[:, None] == grid_col[None, :]
    values = jnp.exp(-distance / 0.25)
    nugget = 0.5
    return values + jnp.where(on_diagonal, jnp.float32(nugget), jnp.float32(0.0))


def setup_inputs(seed: int = 0) -> dict:
    splits = jax.random.split(jax.random.key(seed), 2)
    matrix = draw_matrix(jax.random.fold_in(splits[1], 71), 0)
    return {"matrix": matrix}


def factor_tile(square):
    factor = jnp.linalg.cholesky(square)
    eye_tile = jnp.eye(square.shape[0], dtype=square.dtype)
    inverse = jax.scipy.linalg.solve_triangular(factor, eye_tile, lower=True)
    return (factor, inverse)

def to_columns(stored):
    shaped = stored.reshape(N_ROW, TR, TILE, N_COL, TC, TILE)
    return shaped.transpose(4, 3, 1, 0, 2, 5).reshape(TC * N_COL, TR * N_ROW * TILE, TILE)

def from_columns(columns):
    shaped = columns.reshape(TC, N_COL, TR, N_ROW, TILE, TILE)
    return shaped.transpose(3, 2, 4, 1, 0, 5).reshape(N_ROW * TR * TILE, N_COL * TC * TILE)

def reference(matrix):
    grid_tiles = to_columns(matrix)
    total_rows = grid_tiles.shape[1]
    total_tiles = grid_tiles.shape[0]
    row_tile = jnp.arange(total_rows, dtype=jnp.int32) // TILE
    for panel_step in range(PANELS):
        first_row = panel_step * TILE
        column_old = grid_tiles[panel_step]
        factor, inverse = factor_tile(column_old[first_row:first_row + TILE])
        solved = jnp.dot(column_old.astype(jnp.float32), inverse.T.astype(jnp.float32), precision=lax.Precision.HIGHEST, preferred_element_type=jnp.float32)
        below_step = (row_tile > panel_step)[:, None]
        solved = jnp.where(below_step, solved, jnp.float32(0.0))
        rounded = solved.astype(jnp.bfloat16)

        def update_tile(operands):
            column_block, tile_index = operands
            partner = lax.dynamic_slice_in_dim(rounded, tile_index * TILE, TILE, 0)
            product = jnp.dot(rounded.astype(jnp.float32), partner.T.astype(jnp.float32), preferred_element_type=jnp.float32)
            keep_tile = jnp.logical_and(row_tile >= tile_index, tile_index > panel_step)
            return column_block - jnp.where(keep_tile[:, None], product, jnp.float32(0.0))
        grid_tiles = lax.map(update_tile, (grid_tiles, jnp.arange(total_tiles, dtype=jnp.int32)))
        new_column = column_old.at[first_row:first_row + TILE].set(factor)
        new_column = jnp.where(below_step, solved, new_column)
        grid_tiles = grid_tiles.at[panel_step].set(new_column)
    return from_columns(grid_tiles)
```

```python
import functools

import jax
import jax.numpy as jnp
from jax import lax
from jax.experimental import pallas as pl
from jax.experimental.pallas import tpu as pltpu
from jax.sharding import PartitionSpec as P

TILE = 256
PANELS = 3
SLAB = 32
LANES = 128
MESH = pl.DeviceIdType.MESH


def lane_splat(value, lane):
    return jnp.broadcast_to(value[:, lane : lane + 1], value.shape)


def row_splat(value, row):
    return jnp.broadcast_to(value[row : row + 1, :], value.shape)


def eliminate(tiles):
    row = lax.broadcasted_iota(jnp.int32, tiles[0].shape, 0)
    for j in range(0, SLAB, 2):
        c1, c2 = lane_splat(tiles[0], j), lane_splat(tiles[0], j + 1)
        a, b, d = row_splat(c1, j), row_splat(c1, j + 1), row_splat(c2, j + 1)
        ra = 1.0 / a
        rest = 1.0 / (a * d - b * b)
        ratio = b * ra
        m1 = jnp.where(row > j, c1 * ra, 0.0)
        m2 = jnp.where(row > j + 1, (c2 - c1 * ratio) * (a * rest), 0.0)
        new = []
        for tile in tiles:
            r1 = row_splat(tile, j)
            r2 = row_splat(tile, j + 1) - ratio * r1
            new.append(tile - m1 * r1 - m2 * r2)
        tiles = new
    lane = lax.broadcasted_iota(jnp.int32, tiles[0].shape, 1)
    pivots = jnp.sum(jnp.where(lane == row, tiles[0], 0.0), axis=1, keepdims=True)
    scale = lax.rsqrt(jnp.broadcast_to(pivots, tiles[0].shape))
    return [tile * scale for tile in tiles[1:]]


def down_product(left, right):
    return lax.dot_general(
        left,
        right,
        (((0,), (0,)), ((), ())),
        precision=lax.Precision.HIGHEST,
        preferred_element_type=jnp.float32,
    )


def factor_tile(square, inverse, upper):
    full = (TILE, TILE)
    eye = lax.broadcasted_iota(jnp.int32, full, 0) == lax.broadcasted_iota(jnp.int32, full, 1)
    inverse[...] = jnp.where(eye, 1.0, 0.0)
    for half in range(TILE // LANES):
        base = half * LANES
        width = TILE - base

        def block(index, _, base=base, width=width):
            shift = pl.multiple_of(index * SLAB, SLAB)
            rows = pl.ds(pl.multiple_of(base + shift, SLAB), SLAB)
            slab = [square[rows, s : s + LANES] for s in range(base, TILE, LANES)]
            back = [inverse[rows, s : s + LANES] for s in range(0, base + LANES, LANES)]
            pivot = pltpu.roll(slab[0], lax.rem(LANES - shift, LANES), 1)
            done = eliminate([pivot] + slab + back)
            top = jnp.concatenate(done[: len(slab)], axis=1) if len(slab) > 1 else done[0]
            low = done[len(slab) :]
            low = jnp.concatenate(low, axis=1) if len(low) > 1 else low[0]
            lane = lax.broadcasted_iota(jnp.int32, (SLAB, width), 1)
            row = lax.broadcasted_iota(jnp.int32, (SLAB, width), 0) + shift
            top = jnp.where(lane >= row, top, 0.0)
            after = jnp.where(lane >= shift + SLAB, top, 0.0)
            upper[rows, base:] = top
            if base:
                upper[rows, :base] = jnp.zeros((SLAB, base), jnp.float32)
            inverse[rows, : base + LANES] = low
            square[base:, base:] -= down_product(after, top)
            inverse[base:, : base + LANES] -= down_product(after, low)
            return 0

        lax.fori_loop(0, LANES // SLAB, block, 0)


def kernel(
    row_count,
    col_count,
    matrix,
    out,
    block,
    rounded,
    across,
    inverses,
    square,
    upper,
    load_sem,
    inv_send,
    inv_recv,
    rows_send,
    rows_recv,
    across_send,
    across_recv,
):
    row, col = lax.axis_index("row"), lax.axis_index("col")
    tiles_down = block.shape[0] // TILE
    tiles_across = block.shape[1] // TILE
    load = pltpu.make_async_copy(matrix, block, load_sem)
    load.start()

    barrier = pltpu.get_barrier_semaphore()
    for step in range(1, row_count):
        other = lax.rem(row + step, row_count)
        pl.semaphore_signal(barrier, inc=1, device_id=(other, col), device_id_type=MESH)
    twin = col + 1 - 2 * lax.rem(col, 2)
    pl.semaphore_signal(barrier, inc=1, device_id=(row, twin), device_id_type=MESH)
    has_up = col + 2 < col_count
    has_down = col >= 2

    @pl.when(has_up)
    def _():
        pl.semaphore_signal(barrier, inc=1, device_id=(row, col + 2), device_id_type=MESH)

    @pl.when(has_down)
    def _():
        pl.semaphore_signal(barrier, inc=1, device_id=(row, col - 2), device_id_type=MESH)

    pl.semaphore_wait(barrier, row_count + has_up.astype(jnp.int32) + has_down.astype(jnp.int32))
    load.wait()

    def tile_rows(t):
        return pl.ds(pl.multiple_of(t * TILE, TILE), TILE)

    def inverse_copy(k, step):
        return pltpu.make_async_remote_copy(
            src_ref=inverses.at[k],
            dst_ref=inverses.at[k],
            send_sem=inv_send.at[k, step],
            recv_sem=inv_recv.at[k],
            device_id=(lax.rem(row + step, row_count), col),
            device_id_type=MESH,
        )

    def rows_copy(k, t, way, target):
        return pltpu.make_async_remote_copy(
            src_ref=rounded.at[k, t],
            dst_ref=rounded.at[k, t],
            send_sem=rows_send.at[k, t, way],
            recv_sem=rows_recv.at[k, t],
            device_id=(row, target),
            device_id_type=MESH,
        )

    def across_copy(k, u, step):
        return pltpu.make_async_remote_copy(
            src_ref=rounded.at[k, (u * col_count + col) // row_count],
            dst_ref=across.at[k, u],
            send_sem=across_send.at[k, u, step],
            recv_sem=across_recv.at[k, u],
            device_id=(lax.rem(row + step, row_count), col),
            device_id_type=MESH,
        )

    holds_across = row == lax.rem(col, row_count)

    def sends(k):
        in_lane = lax.rem(col + k, 2) == 0
        up = jnp.logical_and(in_lane, jnp.logical_and(col >= k, has_up))
        down = jnp.logical_and(in_lane, jnp.logical_and(col <= k, has_down))
        return ((in_lane, twin), (up, col + 2), (down, col - 2))

    def pass_on(k, t):
        for way, (do, target) in enumerate(sends(k)):

            @pl.when(do)
            def _(way=way, target=target):
                rows_copy(k, t, way, target).start()

    def send_across(k, u):
        for step in range(1, row_count):
            across_copy(k, u, step).start()

    def update(k, u, t, partner):
        i, j = t * row_count + row, u * col_count + col

        @pl.when(jnp.logical_and(i >= j, j > k))
        def _():
            product = lax.dot_general(
                rounded[k, t],
                partner,
                (((1,), (1,)), ((), ())),
                preferred_element_type=jnp.float32,
            )
            block[tile_rows(t), u * TILE : (u + 1) * TILE] -= product

    def update_column(k, u, first):
        @pl.when(holds_across)
        def _():
            across[k, u] = rounded[k, (u * col_count + col) // row_count]

        @pl.when(jnp.logical_not(holds_across))
        def _():
            across_copy(k, u, 1).wait_recv()

        def one(t, _):
            update(k, u, t, across[k, u])
            return 0

        lax.fori_loop(first, tiles_down, one, 0)

    def panel(k, _):
        last = k - 1
        ahead = jnp.logical_and(row == k, col == k)
        later = jnp.logical_and(ahead, k > 0)

        @pl.when(later)
        def _():
            rows_copy(last, 0, 0, twin).wait_recv()
            send_across(last, 0)
            update(last, 0, 0, rounded[last, 0])

        @pl.when(jnp.logical_and(ahead, k < PANELS))
        def _():
            square[...] = block[0:TILE, 0:TILE]
            factor_tile(square, inverses.at[k], upper)
            for step in range(1, row_count):
                inverse_copy(k, step).start()
            block[0:TILE, 0:TILE] = upper[...].T

        @pl.when(k > 0)
        def _():
            @pl.when(col != last)
            def _():
                def receive(t, _):
                    rows_copy(last, t, 0, twin).wait_recv()
                    pass_on(last, t)
                    return 0

                lax.fori_loop(later.astype(jnp.int32), tiles_down, receive, 0)

            @pl.when(holds_across)
            def _():
                @pl.when(jnp.logical_not(later))
                def _():
                    send_across(last, 0)

                for u in range(1, tiles_across):
                    send_across(last, u)

            update_column(last, 0, later.astype(jnp.int32))

        @pl.when(jnp.logical_and(col == k, k < PANELS))
        def _():
            @pl.when(row != k)
            def _():
                inverse_copy(k, 1).wait_recv()

            def solve(t, _):
                below = t * row_count + row > k

                @pl.when(below)
                def _():
                    solved = lax.dot_general(
                        block[tile_rows(t), 0:TILE],
                        inverses[k],
                        (((1,), (1,)), ((), ())),
                        precision=lax.Precision.HIGHEST,
                        preferred_element_type=jnp.float32,
                    )
                    block[tile_rows(t), 0:TILE] = solved
                    rounded[k, t] = solved.astype(jnp.bfloat16)

                @pl.when(jnp.logical_not(below))
                def _():
                    rounded[k, t] = jnp.zeros((TILE, TILE), jnp.bfloat16)

                pass_on(k, t)
                return 0

            lax.fori_loop(0, tiles_down, solve, 0)

        @pl.when(k > 0)
        def _():
            for u in range(1, tiles_across):
                update_column(last, u, 0)

        return 0

    lax.fori_loop(0, PANELS + 1, panel, 0)

    store = pltpu.make_async_copy(block, out, load_sem)
    store.start()

    def finish(k, _):
        @pl.when(jnp.logical_and(row == k, col == k))
        def _():
            for step in range(1, row_count):
                inverse_copy(k, step).wait_send()

        def rows_done(t, _):
            for way, (do, target) in enumerate(sends(k)):

                @pl.when(do)
                def _(way=way, target=target):
                    rows_copy(k, t, way, target).wait_send()

            return 0

        lax.fori_loop(0, tiles_down, rows_done, 0)

        @pl.when(holds_across)
        def _():
            for u in range(tiles_across):
                for step in range(1, row_count):
                    across_copy(k, u, step).wait_send()

        return 0

    lax.fori_loop(0, PANELS, finish, 0)
    store.wait()


def on_device(row_count, col_count, matrix):
    tiles_down = matrix.shape[0] // TILE
    tiles_across = matrix.shape[1] // TILE
    square = (TILE, TILE)
    return pl.pallas_call(
        functools.partial(kernel, row_count, col_count),
        out_shape=jax.ShapeDtypeStruct(matrix.shape, jnp.float32),
        in_specs=[pl.BlockSpec(memory_space=pl.ANY)],
        out_specs=pl.BlockSpec(memory_space=pl.ANY),
        scratch_shapes=[
            pltpu.VMEM(matrix.shape, jnp.float32),
            pltpu.VMEM((PANELS, tiles_down) + square, jnp.bfloat16),
            pltpu.VMEM((PANELS, tiles_across) + square, jnp.bfloat16),
            pltpu.VMEM((PANELS,) + square, jnp.float32),
            pltpu.VMEM(square, jnp.float32),
            pltpu.VMEM(square, jnp.float32),
            pltpu.SemaphoreType.DMA,
            pltpu.SemaphoreType.DMA((PANELS, row_count)),
            pltpu.SemaphoreType.DMA((PANELS,)),
            pltpu.SemaphoreType.DMA((PANELS, tiles_down, 3)),
            pltpu.SemaphoreType.DMA((PANELS, tiles_down)),
            pltpu.SemaphoreType.DMA((PANELS, tiles_across, row_count)),
            pltpu.SemaphoreType.DMA((PANELS, tiles_across)),
        ],
        compiler_params=pltpu.CompilerParams(
            collective_id=0, has_side_effects=True, vmem_limit_bytes=40 * 1024 * 1024
        ),
        name="panels",
    )(matrix)


def solution(mesh):
    return jax.shard_map(
        functools.partial(on_device, mesh.shape["row"], mesh.shape["col"]),
        mesh=mesh,
        in_specs=(P("row", "col"),),
        out_specs=P("row", "col"),
        check_vma=False,
    )
```

```python
import functools

import jax
import jax.numpy as jnp
from jax import lax
from jax.experimental import pallas as pl
from jax.experimental.pallas import tpu as pltpu
from jax.sharding import PartitionSpec as P

TILE = 256
PANELS = 3
SLAB = 32
GROUP = 8
LANES = 128
MESH = pl.DeviceIdType.MESH


def lane_splat(value, lane):
    return jnp.broadcast_to(value[:, lane : lane + 1], value.shape)


def row_splat(value, row):
    return jnp.broadcast_to(value[row : row + 1, :], value.shape)


def eliminate(tiles):
    finished = [[] for _ in tiles]
    for start in range(0, SLAB, GROUP):
        columns = [lane_splat(tiles[0], start + q) for q in range(GROUP)]
        row = lax.broadcasted_iota(jnp.int32, tiles[0].shape, 0)
        for j in range(0, GROUP, 2):
            c1, c2 = columns[j], columns[j + 1]
            a, b, d = row_splat(c1, j), row_splat(c1, j + 1), row_splat(c2, j + 1)
            ra = 1.0 / a
            rest = a / (a * d - b * b)
            ratio = b * ra
            m1 = jnp.where(row > j, c1 * ra, 0.0)
            m2 = jnp.where(row > j + 1, (c2 - c1 * ratio) * rest, 0.0)
            for q in range(j + 2, GROUP):
                x1 = row_splat(c1, q)
                x2 = row_splat(c2, q) - ratio * x1
                columns[q] = columns[q] - m1 * x1 - m2 * x2
            new = []
            for tile in tiles:
                r1 = row_splat(tile, j)
                r2 = row_splat(tile, j + 1) - ratio * r1
                new.append(tile - m1 * r1 - m2 * r2)
            tiles = new
        for kept, tile in zip(finished, tiles):
            kept.append(tile[:GROUP])
        tiles = [tile[GROUP:] for tile in tiles]
    tiles = [jnp.concatenate(kept, axis=0) for kept in finished]
    row = lax.broadcasted_iota(jnp.int32, tiles[0].shape, 0)
    lane = lax.broadcasted_iota(jnp.int32, tiles[0].shape, 1)
    pivots = jnp.sum(jnp.where(lane == row, tiles[0], 0.0), axis=1, keepdims=True)
    scale = lax.rsqrt(jnp.broadcast_to(pivots, tiles[0].shape))
    return [tile * scale for tile in tiles[1:]]


def precise_product(left, right):
    return jnp.dot(
        left,
        right,
        precision=lax.Precision.HIGHEST,
        preferred_element_type=jnp.float32,
    )


def factor_tile(square, inverse, upper):
    full = (TILE, TILE)
    eye = lax.broadcasted_iota(jnp.int32, full, 0) == lax.broadcasted_iota(jnp.int32, full, 1)
    inverse[...] = jnp.where(eye, 1.0, 0.0)
    upper[...] = jnp.zeros(full, jnp.float32)
    for first in range(0, TILE, SLAB):
        base = first // LANES * LANES
        reach = base + LANES
        shift = first - base
        rows = slice(first, first + SLAB)
        slab = [square[rows, s : s + LANES] for s in range(base, TILE, LANES)]
        back = [inverse[rows, s : s + LANES] for s in range(0, reach, LANES)]
        pivot = pltpu.roll(slab[0], LANES - shift, 1) if shift else slab[0]
        done = eliminate([pivot] + slab + back)
        top = jnp.concatenate(done[: len(slab)], axis=1) if len(slab) > 1 else done[0]
        low = done[len(slab) :]
        low = jnp.concatenate(low, axis=1) if len(low) > 1 else low[0]
        lane = lax.broadcasted_iota(jnp.int32, top.shape, 1)
        row = lax.broadcasted_iota(jnp.int32, top.shape, 0) + shift
        top = jnp.where(lane >= row, top, 0.0)
        upper[rows, base:] = top
        inverse[rows, :reach] = low
        flipped = top.T
        for near, far in ((first + SLAB, first + 2 * SLAB), (first + 2 * SLAB, TILE)):
            if near < far <= TILE:
                left = flipped[near - base : far - base]
                square[near:far, base:] -= precise_product(left, top)
                inverse[near:far, :reach] -= precise_product(left, low)


def kernel(
    row_count,
    col_count,
    matrix,
    out,
    block,
    rounded,
    across,
    inverses,
    square,
    upper,
    load_sem,
    inv_send,
    inv_recv,
    rows_send,
    rows_recv,
    across_send,
    across_recv,
):
    row, col = lax.axis_index("row"), lax.axis_index("col")
    tiles_down = block.shape[0] // TILE
    tiles_across = block.shape[1] // TILE
    load = pltpu.make_async_copy(matrix, block, load_sem)
    load.start()

    barrier = pltpu.get_barrier_semaphore()
    for step in range(1, row_count):
        other = lax.rem(row + step, row_count)
        pl.semaphore_signal(barrier, inc=1, device_id=(other, col), device_id_type=MESH)
    twin = col + 1 - 2 * lax.rem(col, 2)
    pl.semaphore_signal(barrier, inc=1, device_id=(row, twin), device_id_type=MESH)
    has_up = col + 2 < col_count
    has_down = col >= 2

    @pl.when(has_up)
    def _():
        pl.semaphore_signal(barrier, inc=1, device_id=(row, col + 2), device_id_type=MESH)

    @pl.when(has_down)
    def _():
        pl.semaphore_signal(barrier, inc=1, device_id=(row, col - 2), device_id_type=MESH)

    pl.semaphore_wait(barrier, row_count + has_up.astype(jnp.int32) + has_down.astype(jnp.int32))
    load.wait()

    def tile_rows(t):
        return pl.ds(pl.multiple_of(t * TILE, TILE), TILE)

    def inverse_copy(k, step):
        return pltpu.make_async_remote_copy(
            src_ref=inverses.at[k],
            dst_ref=inverses.at[k],
            send_sem=inv_send.at[k, step],
            recv_sem=inv_recv.at[k],
            device_id=(lax.rem(row + step, row_count), col),
            device_id_type=MESH,
        )

    def rows_copy(k, t, way, target):
        return pltpu.make_async_remote_copy(
            src_ref=rounded.at[k, t],
            dst_ref=rounded.at[k, t],
            send_sem=rows_send.at[k, t, way],
            recv_sem=rows_recv.at[k, t],
            device_id=(row, target),
            device_id_type=MESH,
        )

    def across_copy(k, u, step):
        return pltpu.make_async_remote_copy(
            src_ref=rounded.at[k, (u * col_count + col) // row_count],
            dst_ref=across.at[k, u],
            send_sem=across_send.at[k, u, step],
            recv_sem=across_recv.at[k, u],
            device_id=(lax.rem(row + step, row_count), col),
            device_id_type=MESH,
        )

    holds_across = row == lax.rem(col, row_count)

    def sends(k, t):
        split = k == PANELS - 1
        odd = jnp.where(split, lax.rem(t, 2), 0)
        in_lane = lax.rem(col + k + odd, 2) == 0
        own_twin = k + 1 - 2 * lax.rem(k, 2)
        place, source = col // 2, k // 2
        up = jnp.logical_and(in_lane, jnp.logical_and(place >= source, has_up))
        down = jnp.logical_and(in_lane, jnp.logical_and(place <= source, has_down))
        returns = jnp.logical_and(split, jnp.logical_and(odd == 0, col == own_twin + 2))
        first = jnp.logical_and(col == k, jnp.logical_or(jnp.logical_not(split), odd == 1))
        cross = jnp.logical_or(first, jnp.logical_and(in_lane, place != source))
        return ((cross, twin), (up, col + 2), (jnp.logical_or(down, returns), col - 2))

    def pass_on(k, t):
        for way, (do, target) in enumerate(sends(k, t)):

            @pl.when(do)
            def _(way=way, target=target):
                rows_copy(k, t, way, target).start()

    def send_across(k, u):
        for step in range(1, row_count):
            across_copy(k, u, step).start()

    def update(k, u, t, partner):
        i, j = t * row_count + row, u * col_count + col

        @pl.when(jnp.logical_and(i >= j, j > k))
        def _():
            product = lax.dot_general(
                rounded[k, t],
                partner,
                (((1,), (1,)), ((), ())),
                preferred_element_type=jnp.float32,
            )
            block[tile_rows(t), u * TILE : (u + 1) * TILE] -= product

    def update_column(k, u, first):
        @pl.when(holds_across)
        def _():
            across[k, u] = rounded[k, (u * col_count + col) // row_count]

        @pl.when(jnp.logical_not(holds_across))
        def _():
            across_copy(k, u, 1).wait_recv()

        def one(t, _):
            update(k, u, t, across[k, u])
            return 0

        lax.fori_loop(first, tiles_down, one, 0)

    def panel(k, _):
        last = k - 1
        ahead = jnp.logical_and(row == k, col == k)
        later = jnp.logical_and(ahead, k > 0)

        @pl.when(later)
        def _():
            rows_copy(last, 0, 0, twin).wait_recv()
            send_across(last, 0)
            update(last, 0, 0, rounded[last, 0])

        @pl.when(jnp.logical_and(ahead, k < PANELS))
        def _():
            square[...] = block[0:TILE, 0:TILE]
            factor_tile(square, inverses.at[k], upper)
            for step in range(1, row_count):
                inverse_copy(k, step).start()
            block[0:TILE, 0:TILE] = upper[...].T

        @pl.when(k > 0)
        def _():
            @pl.when(col != last)
            def _():
                def receive(t, _):
                    rows_copy(last, t, 0, twin).wait_recv()
                    pass_on(last, t)
                    return 0

                lax.fori_loop(later.astype(jnp.int32), tiles_down, receive, 0)

            @pl.when(holds_across)
            def _():
                @pl.when(jnp.logical_not(later))
                def _():
                    send_across(last, 0)

                for u in range(1, tiles_across):
                    send_across(last, u)

            update_column(last, 0, later.astype(jnp.int32))

        @pl.when(jnp.logical_and(col == k, k < PANELS))
        def _():
            @pl.when(row != k)
            def _():
                inverse_copy(k, 1).wait_recv()

            def solve(t, _):
                below = t * row_count + row > k

                @pl.when(below)
                def _():
                    solved = lax.dot_general(
                        block[tile_rows(t), 0:TILE],
                        inverses[k],
                        (((1,), (1,)), ((), ())),
                        precision=lax.Precision.HIGHEST,
                        preferred_element_type=jnp.float32,
                    )
                    block[tile_rows(t), 0:TILE] = solved
                    rounded[k, t] = solved.astype(jnp.bfloat16)

                @pl.when(jnp.logical_not(below))
                def _():
                    rounded[k, t] = jnp.zeros((TILE, TILE), jnp.bfloat16)

                pass_on(k, t)
                return 0

            lax.fori_loop(0, tiles_down, solve, 0)

        @pl.when(k > 0)
        def _():
            for u in range(1, tiles_across):
                update_column(last, u, 0)

        return 0

    lax.fori_loop(0, PANELS + 1, panel, 0)

    store = pltpu.make_async_copy(block, out, load_sem)
    store.start()

    def finish(k, _):
        @pl.when(jnp.logical_and(row == k, col == k))
        def _():
            for step in range(1, row_count):
                inverse_copy(k, step).wait_send()

        def rows_done(t, _):
            for way, (do, target) in enumerate(sends(k, t)):

                @pl.when(do)
                def _(way=way, target=target):
                    rows_copy(k, t, way, target).wait_send()

            return 0

        lax.fori_loop(0, tiles_down, rows_done, 0)

        @pl.when(holds_across)
        def _():
            for u in range(tiles_across):
                for step in range(1, row_count):
                    across_copy(k, u, step).wait_send()

        return 0

    lax.fori_loop(0, PANELS, finish, 0)
    store.wait()


def on_device(row_count, col_count, matrix):
    tiles_down = matrix.shape[0] // TILE
    tiles_across = matrix.shape[1] // TILE
    square = (TILE, TILE)
    return pl.pallas_call(
        functools.partial(kernel, row_count, col_count),
        out_shape=jax.ShapeDtypeStruct(matrix.shape, jnp.float32),
        in_specs=[pl.BlockSpec(memory_space=pl.ANY)],
        out_specs=pl.BlockSpec(memory_space=pl.ANY),
        scratch_shapes=[
            pltpu.VMEM(matrix.shape, jnp.float32),
            pltpu.VMEM((PANELS, tiles_down) + square, jnp.bfloat16),
            pltpu.VMEM((PANELS, tiles_across) + square, jnp.bfloat16),
            pltpu.VMEM((PANELS,) + square, jnp.float32),
            pltpu.VMEM(square, jnp.float32),
            pltpu.VMEM(square, jnp.float32),
            pltpu.SemaphoreType.DMA,
            pltpu.SemaphoreType.DMA((PANELS, row_count)),
            pltpu.SemaphoreType.DMA((PANELS,)),
            pltpu.SemaphoreType.DMA((PANELS, tiles_down, 3)),
            pltpu.SemaphoreType.DMA((PANELS, tiles_down)),
            pltpu.SemaphoreType.DMA((PANELS, tiles_across, row_count)),
            pltpu.SemaphoreType.DMA((PANELS, tiles_across)),
        ],
        compiler_params=pltpu.CompilerParams(
            collective_id=0, has_side_effects=True, vmem_limit_bytes=60 * 1024 * 1024
        ),
        name="panels",
    )(matrix)


def solution(mesh):
    return jax.shard_map(
        functools.partial(on_device, mesh.shape["row"], mesh.shape["col"]),
        mesh=mesh,
        in_specs=(P("row", "col"),),
        out_specs=P("row", "col"),
        check_vma=False,
    )
```

```python
import functools

import jax
import jax.numpy as jnp
from jax import lax
from jax.experimental import pallas as pl
from jax.experimental.pallas import tpu as pltpu
from jax.sharding import PartitionSpec as P

TILE = 256
PANELS = 3
SLAB = 32
GROUP = 8
LANES = 128
MESH = pl.DeviceIdType.MESH


def lane_splat(value, lane):
    return jnp.broadcast_to(value[:, lane : lane + 1], value.shape)


def row_splat(value, row):
    return jnp.broadcast_to(value[row : row + 1, :], value.shape)


def eliminate(tiles):
    finished = [[] for _ in tiles]
    for start in range(0, SLAB, GROUP):
        columns = [lane_splat(tiles[0], start + q) for q in range(GROUP)]
        row = lax.broadcasted_iota(jnp.int32, tiles[0].shape, 0)
        for j in range(0, GROUP, 2):
            c1, c2 = columns[j], columns[j + 1]
            a, b, d = row_splat(c1, j), row_splat(c1, j + 1), row_splat(c2, j + 1)
            ra = 1.0 / a
            rest = a / (a * d - b * b)
            ratio = b * ra
            m1 = jnp.where(row > j, c1 * ra, 0.0)
            m2 = jnp.where(row > j + 1, (c2 - c1 * ratio) * rest, 0.0)
            for q in range(j + 2, GROUP):
                x1 = row_splat(c1, q)
                x2 = row_splat(c2, q) - ratio * x1
                columns[q] = columns[q] - m1 * x1 - m2 * x2
            new = []
            for tile in tiles:
                r1 = row_splat(tile, j)
                r2 = row_splat(tile, j + 1) - ratio * r1
                new.append(tile - m1 * r1 - m2 * r2)
            tiles = new
        for kept, tile in zip(finished, tiles):
            kept.append(tile[:GROUP])
        tiles = [tile[GROUP:] for tile in tiles]
    tiles = [jnp.concatenate(kept, axis=0) for kept in finished]
    row = lax.broadcasted_iota(jnp.int32, tiles[0].shape, 0)
    lane = lax.broadcasted_iota(jnp.int32, tiles[0].shape, 1)
    pivots = jnp.sum(jnp.where(lane == row, tiles[0], 0.0), axis=1, keepdims=True)
    scale = lax.rsqrt(jnp.broadcast_to(pivots, tiles[0].shape))
    return [tile * scale for tile in tiles[1:]]


def precise_product(left, right):
    return jnp.dot(
        left,
        right,
        precision=lax.Precision.HIGHEST,
        preferred_element_type=jnp.float32,
    )


def factor_tile(square, inverse, upper):
    full = (TILE, TILE)
    eye = lax.broadcasted_iota(jnp.int32, full, 0) == lax.broadcasted_iota(jnp.int32, full, 1)
    inverse[...] = jnp.where(eye, 1.0, 0.0)
    upper[...] = jnp.zeros(full, jnp.float32)
    for first in range(0, TILE, SLAB):
        base = first // LANES * LANES
        reach = base + LANES
        shift = first - base
        rows = slice(first, first + SLAB)
        slab = [square[rows, s : s + LANES] for s in range(base, TILE, LANES)]
        back = [inverse[rows, s : s + LANES] for s in range(0, reach, LANES)]
        pivot = pltpu.roll(slab[0], LANES - shift, 1) if shift else slab[0]
        done = eliminate([pivot] + slab + back)
        top = jnp.concatenate(done[: len(slab)], axis=1) if len(slab) > 1 else done[0]
        low = done[len(slab) :]
        low = jnp.concatenate(low, axis=1) if len(low) > 1 else low[0]
        lane = lax.broadcasted_iota(jnp.int32, top.shape, 1)
        row = lax.broadcasted_iota(jnp.int32, top.shape, 0) + shift
        top = jnp.where(lane >= row, top, 0.0)
        upper[rows, base:] = top
        inverse[rows, :reach] = low
        flipped = top.T
        for near, far in ((first + SLAB, first + 2 * SLAB), (first + 2 * SLAB, TILE)):
            if near < far <= TILE:
                left = flipped[near - base : far - base]
                square[near:far, base:] -= precise_product(left, top)
                inverse[near:far, :reach] -= precise_product(left, low)


def kernel(
    row_count,
    col_count,
    matrix,
    out,
    block,
    rounded,
    across,
    inverses,
    square,
    upper,
    load_sem,
    inv_send,
    inv_recv,
    rows_send,
    rows_recv,
    across_send,
    across_recv,
):
    row, col = lax.axis_index("row"), lax.axis_index("col")
    tiles_down = block.shape[0] // TILE
    tiles_across = block.shape[1] // TILE
    load = pltpu.make_async_copy(matrix, block, load_sem)
    load.start()

    barrier = pltpu.get_barrier_semaphore()
    for step in range(1, row_count):
        other = lax.rem(row + step, row_count)
        pl.semaphore_signal(barrier, inc=1, device_id=(other, col), device_id_type=MESH)
    twin = col + 1 - 2 * lax.rem(col, 2)
    pl.semaphore_signal(barrier, inc=1, device_id=(row, twin), device_id_type=MESH)
    has_up = col + 2 < col_count
    has_down = col >= 2

    @pl.when(has_up)
    def _():
        pl.semaphore_signal(barrier, inc=1, device_id=(row, col + 2), device_id_type=MESH)

    @pl.when(has_down)
    def _():
        pl.semaphore_signal(barrier, inc=1, device_id=(row, col - 2), device_id_type=MESH)

    pl.semaphore_wait(barrier, row_count + has_up.astype(jnp.int32) + has_down.astype(jnp.int32))
    load.wait()

    def tile_rows(t):
        return pl.ds(pl.multiple_of(t * TILE, TILE), TILE)

    def inverse_copy(k, step):
        return pltpu.make_async_remote_copy(
            src_ref=inverses.at[k],
            dst_ref=inverses.at[k],
            send_sem=inv_send.at[k, step],
            recv_sem=inv_recv.at[k],
            device_id=(lax.rem(row + step, row_count), col),
            device_id_type=MESH,
        )

    def rows_copy(k, t, way, target):
        return pltpu.make_async_remote_copy(
            src_ref=rounded.at[k, t],
            dst_ref=rounded.at[k, t],
            send_sem=rows_send.at[k, t, way],
            recv_sem=rows_recv.at[k, t],
            device_id=(row, target),
            device_id_type=MESH,
        )

    def across_row(u):
        return (u * col_count + col) // row_count

    def across_copy(k, u, step):
        return pltpu.make_async_remote_copy(
            src_ref=rounded.at[k, across_row(u)],
            dst_ref=across.at[k, u],
            send_sem=across_send.at[k, u, step],
            recv_sem=across_recv.at[k, u],
            device_id=(lax.rem(row + step, row_count), col),
            device_id_type=MESH,
        )

    holds_across = row == lax.rem(col, row_count)

    def sends(k, t):
        split = k == PANELS - 1
        odd = jnp.where(split, lax.rem(t, 2), 0)
        in_lane = lax.rem(col + k + odd, 2) == 0
        own_twin = k + 1 - 2 * lax.rem(k, 2)
        place, source = col // 2, k // 2
        up = jnp.logical_and(in_lane, jnp.logical_and(place >= source, has_up))
        down = jnp.logical_and(in_lane, jnp.logical_and(place <= source, has_down))
        returns = jnp.logical_and(split, jnp.logical_and(odd == 0, col == own_twin + 2))
        first = jnp.logical_and(col == k, jnp.logical_or(jnp.logical_not(split), odd == 1))
        cross = jnp.logical_or(first, jnp.logical_and(in_lane, place != source))
        return ((cross, twin), (up, col + 2), (jnp.logical_or(down, returns), col - 2))

    def arrival(k, step):
        own = lax.rem(col + k, 2)
        end = step == tiles_down - 1
        ahead = jnp.logical_or(step == 0, jnp.logical_and(lax.rem(step, 2) == 1, step < tiles_down - 1))
        place = jnp.where(
            ahead, (step + 1) // 2, jnp.where(end, tiles_down // 2 - 1, (step + tiles_down - 2) // 2 - tiles_down // 2)
        )
        mixed = 2 * place + jnp.where(ahead, own, 1 - own)
        return jnp.where(k == PANELS - 1, mixed, step)

    def pass_on(k, t):
        for way, (do, target) in enumerate(sends(k, t)):

            @pl.when(do)
            def _(way=way, target=target):
                rows_copy(k, t, way, target).start()

    def send_across(k, u):
        for step in range(1, row_count):
            across_copy(k, u, step).start()

    def update(k, u, t, partner):
        i, j = t * row_count + row, u * col_count + col

        @pl.when(jnp.logical_and(i >= j, j > k))
        def _():
            product = lax.dot_general(
                rounded[k, t],
                partner,
                (((1,), (1,)), ((), ())),
                preferred_element_type=jnp.float32,
            )
            block[tile_rows(t), u * TILE : (u + 1) * TILE] -= product

    def update_column(k, u, first):
        @pl.when(holds_across)
        def _():
            across[k, u] = rounded[k, across_row(u)]

        @pl.when(jnp.logical_not(holds_across))
        def _():
            across_copy(k, u, 1).wait_recv()

        def one(t, _):
            update(k, u, t, across[k, u])
            return 0

        lax.fori_loop(first, tiles_down, one, 0)

    def panel(k, _):
        last = k - 1
        ahead = jnp.logical_and(k < PANELS, jnp.logical_and(row == k, col == k))
        later = jnp.logical_and(ahead, k > 0)

        @pl.when(later)
        def _():
            rows_copy(last, 0, 0, twin).wait_recv()
            send_across(last, 0)
            update(last, 0, 0, rounded[last, 0])

        @pl.when(ahead)
        def _():
            square[...] = block[0:TILE, 0:TILE]
            factor_tile(square, inverses.at[k], upper)
            for step in range(1, row_count):
                inverse_copy(k, step).start()
            block[0:TILE, 0:TILE] = upper[...].T

        @pl.when(k > 0)
        def _():
            @pl.when(col != last)
            def _():
                def receive(step, _):
                    t = arrival(last, step)
                    rows_copy(last, t, 0, twin).wait_recv()
                    pass_on(last, t)
                    for u in range(tiles_across):

                        @pl.when(jnp.logical_and(holds_across, t == across_row(u)))
                        def _(u=u):
                            send_across(last, u)

                    return 0

                lax.fori_loop(later.astype(jnp.int32), tiles_down, receive, 0)

            @pl.when(jnp.logical_and(col == last, holds_across))
            def _():
                for u in range(tiles_across):
                    send_across(last, u)

            update_column(last, 0, later.astype(jnp.int32))

        @pl.when(jnp.logical_and(col == k, k < PANELS))
        def _():
            @pl.when(row != k)
            def _():
                inverse_copy(k, 1).wait_recv()

            def solve(t, _):
                below = t * row_count + row > k

                @pl.when(below)
                def _():
                    solved = lax.dot_general(
                        block[tile_rows(t), 0:TILE],
                        inverses[k],
                        (((1,), (1,)), ((), ())),
                        precision=lax.Precision.HIGHEST,
                        preferred_element_type=jnp.float32,
                    )
                    block[tile_rows(t), 0:TILE] = solved
                    rounded[k, t] = solved.astype(jnp.bfloat16)

                @pl.when(jnp.logical_not(below))
                def _():
                    rounded[k, t] = jnp.zeros((TILE, TILE), jnp.bfloat16)

                pass_on(k, t)
                return 0

            lax.fori_loop(0, tiles_down, solve, 0)

        @pl.when(k > 0)
        def _():
            for u in range(1, tiles_across):
                update_column(last, u, 0)

        return 0

    lax.fori_loop(0, PANELS + 1, panel, 0)

    store = pltpu.make_async_copy(block, out, load_sem)
    store.start()

    def finish(k, _):
        @pl.when(jnp.logical_and(row == k, col == k))
        def _():
            for step in range(1, row_count):
                inverse_copy(k, step).wait_send()

        def rows_done(t, _):
            for way, (do, target) in enumerate(sends(k, t)):

                @pl.when(do)
                def _(way=way, target=target):
                    rows_copy(k, t, way, target).wait_send()

            return 0

        lax.fori_loop(0, tiles_down, rows_done, 0)

        @pl.when(holds_across)
        def _():
            for u in range(tiles_across):
                for step in range(1, row_count):
                    across_copy(k, u, step).wait_send()

        return 0

    lax.fori_loop(0, PANELS, finish, 0)
    store.wait()


def on_device(row_count, col_count, matrix):
    tiles_down = matrix.shape[0] // TILE
    tiles_across = matrix.shape[1] // TILE
    square = (TILE, TILE)
    return pl.pallas_call(
        functools.partial(kernel, row_count, col_count),
        out_shape=jax.ShapeDtypeStruct(matrix.shape, jnp.float32),
        in_specs=[pl.BlockSpec(memory_space=pl.ANY)],
        out_specs=pl.BlockSpec(memory_space=pl.ANY),
        scratch_shapes=[
            pltpu.VMEM(matrix.shape, jnp.float32),
            pltpu.VMEM((PANELS, tiles_down) + square, jnp.bfloat16),
            pltpu.VMEM((PANELS, tiles_across) + square, jnp.bfloat16),
            pltpu.VMEM((PANELS,) + square, jnp.float32),
            pltpu.VMEM(square, jnp.float32),
            pltpu.VMEM(square, jnp.float32),
            pltpu.SemaphoreType.DMA,
            pltpu.SemaphoreType.DMA((PANELS, row_count)),
            pltpu.SemaphoreType.DMA((PANELS,)),
            pltpu.SemaphoreType.DMA((PANELS, tiles_down, 3)),
            pltpu.SemaphoreType.DMA((PANELS, tiles_down)),
            pltpu.SemaphoreType.DMA((PANELS, tiles_across, row_count)),
            pltpu.SemaphoreType.DMA((PANELS, tiles_across)),
        ],
        compiler_params=pltpu.CompilerParams(
            collective_id=0, has_side_effects=True, vmem_limit_bytes=40 * 1024 * 1024
        ),
        name="panels",
    )(matrix)


def solution(mesh):
    return jax.shard_map(
        functools.partial(on_device, mesh.shape["row"], mesh.shape["col"]),
        mesh=mesh,
        in_specs=(P("row", "col"),),
        out_specs=P("row", "col"),
        check_vma=False,
    )
```

```python
import functools

import jax
import jax.numpy as jnp
from jax import lax
from jax.experimental import pallas as pl
from jax.experimental.pallas import tpu as pltpu
from jax.sharding import PartitionSpec as P

TILE = 256
PANELS = 3
SLAB = 64
GROUP = 8
LANES = 128
MESH = pl.DeviceIdType.MESH


def lane_splat(value, lane):
    return jnp.broadcast_to(value[:, lane : lane + 1], value.shape)


def row_splat(value, row):
    return jnp.broadcast_to(value[row : row + 1, :], value.shape)


def eliminate(tiles):
    finished = [[] for _ in tiles]
    for start in range(0, SLAB, GROUP):
        columns = [lane_splat(tiles[0], start + q) for q in range(GROUP)]
        row = lax.broadcasted_iota(jnp.int32, tiles[0].shape, 0)
        for j in range(0, GROUP, 2):
            c1, c2 = columns[j], columns[j + 1]
            a, b, d = row_splat(c1, j), row_splat(c1, j + 1), row_splat(c2, j + 1)
            ra = 1.0 / a
            rest = a / (a * d - b * b)
            ratio = b * ra
            m1 = jnp.where(row > j, c1 * ra, 0.0)
            m2 = jnp.where(row > j + 1, (c2 - c1 * ratio) * rest, 0.0)
            for q in range(j + 2, GROUP):
                x1 = row_splat(c1, q)
                x2 = row_splat(c2, q) - ratio * x1
                columns[q] = columns[q] - m1 * x1 - m2 * x2
            new = []
            for tile in tiles:
                r1 = row_splat(tile, j)
                r2 = row_splat(tile, j + 1) - ratio * r1
                new.append(tile - m1 * r1 - m2 * r2)
            tiles = new
        for kept, tile in zip(finished, tiles):
            kept.append(tile[:GROUP])
        tiles = [tile[GROUP:] for tile in tiles]
    tiles = [jnp.concatenate(kept, axis=0) for kept in finished]
    row = lax.broadcasted_iota(jnp.int32, tiles[0].shape, 0)
    lane = lax.broadcasted_iota(jnp.int32, tiles[0].shape, 1)
    pivots = jnp.sum(jnp.where(lane == row, tiles[0], 0.0), axis=1, keepdims=True)
    scale = lax.rsqrt(jnp.broadcast_to(pivots, tiles[0].shape))
    return [tile * scale for tile in tiles[1:]]


def precise_product(left, right):
    return jnp.dot(
        left,
        right,
        precision=lax.Precision.HIGHEST,
        preferred_element_type=jnp.float32,
    )


def factor_tile(square, inverse, upper):
    full = (TILE, TILE)
    eye = lax.broadcasted_iota(jnp.int32, full, 0) == lax.broadcasted_iota(jnp.int32, full, 1)
    inverse[...] = jnp.where(eye, 1.0, 0.0)
    upper[...] = jnp.zeros(full, jnp.float32)
    for first in range(0, TILE, SLAB):
        base = first // LANES * LANES
        reach = base + LANES
        shift = first - base
        rows = slice(first, first + SLAB)
        slab = [square[rows, s : s + LANES] for s in range(base, TILE, LANES)]
        back = [inverse[rows, s : s + LANES] for s in range(0, reach, LANES)]
        pivot = pltpu.roll(slab[0], LANES - shift, 1) if shift else slab[0]
        done = eliminate([pivot] + slab + back)
        top = jnp.concatenate(done[: len(slab)], axis=1) if len(slab) > 1 else done[0]
        low = done[len(slab) :]
        low = jnp.concatenate(low, axis=1) if len(low) > 1 else low[0]
        lane = lax.broadcasted_iota(jnp.int32, top.shape, 1)
        row = lax.broadcasted_iota(jnp.int32, top.shape, 0) + shift
        top = jnp.where(lane >= row, top, 0.0)
        upper[rows, base:] = top
        inverse[rows, :reach] = low
        flipped = top.T
        for near, far in ((first + SLAB, first + 2 * SLAB), (first + 2 * SLAB, TILE)):
            if near < far <= TILE:
                left = flipped[near - base : far - base]
                square[near:far, base:] -= precise_product(left, top)
                inverse[near:far, :reach] -= precise_product(left, low)


def kernel(
    row_count,
    col_count,
    matrix,
    out,
    block,
    rounded,
    across,
    inverses,
    square,
    upper,
    load_sem,
    inv_send,
    inv_recv,
    rows_send,
    rows_recv,
    across_send,
    across_recv,
):
    row, col = lax.axis_index("row"), lax.axis_index("col")
    tiles_down = block.shape[0] // TILE
    tiles_across = block.shape[1] // TILE
    load = pltpu.make_async_copy(matrix, block, load_sem)
    load.start()

    barrier = pltpu.get_barrier_semaphore()
    for step in range(1, row_count):
        other = lax.rem(row + step, row_count)
        pl.semaphore_signal(barrier, inc=1, device_id=(other, col), device_id_type=MESH)
    twin = col + 1 - 2 * lax.rem(col, 2)
    pl.semaphore_signal(barrier, inc=1, device_id=(row, twin), device_id_type=MESH)
    has_up = col + 2 < col_count
    has_down = col >= 2

    @pl.when(has_up)
    def _():
        pl.semaphore_signal(barrier, inc=1, device_id=(row, col + 2), device_id_type=MESH)

    @pl.when(has_down)
    def _():
        pl.semaphore_signal(barrier, inc=1, device_id=(row, col - 2), device_id_type=MESH)

    pl.semaphore_wait(barrier, row_count + has_up.astype(jnp.int32) + has_down.astype(jnp.int32))
    load.wait()

    def tile_rows(t):
        return pl.ds(pl.multiple_of(t * TILE, TILE), TILE)

    def inverse_copy(k, step):
        return pltpu.make_async_remote_copy(
            src_ref=inverses.at[k],
            dst_ref=inverses.at[k],
            send_sem=inv_send.at[k, step],
            recv_sem=inv_recv.at[k],
            device_id=(lax.rem(row + step, row_count), col),
            device_id_type=MESH,
        )

    def rows_copy(k, t, way, target):
        return pltpu.make_async_remote_copy(
            src_ref=rounded.at[k, t],
            dst_ref=rounded.at[k, t],
            send_sem=rows_send.at[k, t, way],
            recv_sem=rows_recv.at[k, t],
            device_id=(row, target),
            device_id_type=MESH,
        )

    def across_row(u):
        return (u * col_count + col) // row_count

    def across_copy(k, u, step):
        return pltpu.make_async_remote_copy(
            src_ref=rounded.at[k, across_row(u)],
            dst_ref=across.at[k, u],
            send_sem=across_send.at[k, u, step],
            recv_sem=across_recv.at[k, u],
            device_id=(lax.rem(row + step, row_count), col),
            device_id_type=MESH,
        )

    holds_across = row == lax.rem(col, row_count)

    def sends(k, t):
        split = k == PANELS - 1
        odd = jnp.where(split, lax.rem(t, 2), 0)
        in_lane = lax.rem(col + k + odd, 2) == 0
        own_twin = k + 1 - 2 * lax.rem(k, 2)
        place, source = col // 2, k // 2
        up = jnp.logical_and(in_lane, jnp.logical_and(place >= source, has_up))
        down = jnp.logical_and(in_lane, jnp.logical_and(place <= source, has_down))
        returns = jnp.logical_and(split, jnp.logical_and(odd == 0, col == own_twin + 2))
        first = jnp.logical_and(col == k, jnp.logical_or(jnp.logical_not(split), odd == 1))
        cross = jnp.logical_or(first, jnp.logical_and(in_lane, place != source))
        return ((cross, twin), (up, col + 2), (jnp.logical_or(down, returns), col - 2))

    def arrival(k, step):
        own = lax.rem(col + k, 2)
        end = step == tiles_down - 1
        ahead = jnp.logical_or(step == 0, jnp.logical_and(lax.rem(step, 2) == 1, step < tiles_down - 1))
        place = jnp.where(
            ahead, (step + 1) // 2, jnp.where(end, tiles_down // 2 - 1, (step + tiles_down - 2) // 2 - tiles_down // 2)
        )
        mixed = 2 * place + jnp.where(ahead, own, 1 - own)
        return jnp.where(k == PANELS - 1, mixed, step)

    def pass_on(k, t):
        for way, (do, target) in enumerate(sends(k, t)):

            @pl.when(do)
            def _(way=way, target=target):
                rows_copy(k, t, way, target).start()

    def send_across(k, u):
        for step in range(1, row_count):
            across_copy(k, u, step).start()

    def update(k, u, t, partner):
        i, j = t * row_count + row, u * col_count + col

        @pl.when(jnp.logical_and(i >= j, j > k))
        def _():
            product = lax.dot_general(
                rounded[k, t],
                partner,
                (((1,), (1,)), ((), ())),
                preferred_element_type=jnp.float32,
            )
            block[tile_rows(t), u * TILE : (u + 1) * TILE] -= product

    def update_column(k, u, first):
        @pl.when(holds_across)
        def _():
            across[k, u] = rounded[k, across_row(u)]

        @pl.when(jnp.logical_not(holds_across))
        def _():
            across_copy(k, u, 1).wait_recv()

        def one(t, _):
            update(k, u, t, across[k, u])
            return 0

        lax.fori_loop(first, tiles_down, one, 0)

    def panel(k, _):
        last = k - 1
        ahead = jnp.logical_and(k < PANELS, jnp.logical_and(row == k, col == k))
        later = jnp.logical_and(ahead, k > 0)

        @pl.when(later)
        def _():
            rows_copy(last, 0, 0, twin).wait_recv()
            send_across(last, 0)
            update(last, 0, 0, rounded[last, 0])

        @pl.when(ahead)
        def _():
            square[...] = block[0:TILE, 0:TILE]
            factor_tile(square, inverses.at[k], upper)
            for step in range(1, row_count):
                inverse_copy(k, step).start()
            block[0:TILE, 0:TILE] = upper[...].T

        @pl.when(k > 0)
        def _():
            @pl.when(col != last)
            def _():
                def receive(step, _):
                    t = arrival(last, step)
                    rows_copy(last, t, 0, twin).wait_recv()
                    pass_on(last, t)
                    for u in range(tiles_across):

                        @pl.when(jnp.logical_and(holds_across, t == across_row(u)))
                        def _(u=u):
                            send_across(last, u)

                    return 0

                lax.fori_loop(later.astype(jnp.int32), tiles_down, receive, 0)

            @pl.when(jnp.logical_and(col == last, holds_across))
            def _():
                for u in range(tiles_across):
                    send_across(last, u)

            update_column(last, 0, later.astype(jnp.int32))

        @pl.when(jnp.logical_and(col == k, k < PANELS))
        def _():
            @pl.when(row != k)
            def _():
                inverse_copy(k, 1).wait_recv()

            def solve(t, _):
                below = t * row_count + row > k

                @pl.when(below)
                def _():
                    solved = lax.dot_general(
                        block[tile_rows(t), 0:TILE],
                        inverses[k],
                        (((1,), (1,)), ((), ())),
                        precision=lax.Precision.HIGHEST,
                        preferred_element_type=jnp.float32,
                    )
                    block[tile_rows(t), 0:TILE] = solved
                    rounded[k, t] = solved.astype(jnp.bfloat16)

                @pl.when(jnp.logical_not(below))
                def _():
                    rounded[k, t] = jnp.zeros((TILE, TILE), jnp.bfloat16)

                pass_on(k, t)
                return 0

            lax.fori_loop(0, tiles_down, solve, 0)

        @pl.when(k > 0)
        def _():
            for u in range(1, tiles_across):
                update_column(last, u, 0)

        return 0

    lax.fori_loop(0, PANELS + 1, panel, 0)

    store = pltpu.make_async_copy(block, out, load_sem)
    store.start()

    def finish(k, _):
        @pl.when(jnp.logical_and(row == k, col == k))
        def _():
            for step in range(1, row_count):
                inverse_copy(k, step).wait_send()

        def rows_done(t, _):
            for way, (do, target) in enumerate(sends(k, t)):

                @pl.when(do)
                def _(way=way, target=target):
                    rows_copy(k, t, way, target).wait_send()

            return 0

        lax.fori_loop(0, tiles_down, rows_done, 0)

        @pl.when(holds_across)
        def _():
            for u in range(tiles_across):
                for step in range(1, row_count):
                    across_copy(k, u, step).wait_send()

        return 0

    lax.fori_loop(0, PANELS, finish, 0)
    store.wait()


def on_device(row_count, col_count, matrix):
    tiles_down = matrix.shape[0] // TILE
    tiles_across = matrix.shape[1] // TILE
    square = (TILE, TILE)
    return pl.pallas_call(
        functools.partial(kernel, row_count, col_count),
        out_shape=jax.ShapeDtypeStruct(matrix.shape, jnp.float32),
        in_specs=[pl.BlockSpec(memory_space=pl.ANY)],
        out_specs=pl.BlockSpec(memory_space=pl.ANY),
        scratch_shapes=[
            pltpu.VMEM(matrix.shape, jnp.float32),
            pltpu.VMEM((PANELS, tiles_down) + square, jnp.bfloat16),
            pltpu.VMEM((PANELS, tiles_across) + square, jnp.bfloat16),
            pltpu.VMEM((PANELS,) + square, jnp.float32),
            pltpu.VMEM(square, jnp.float32),
            pltpu.VMEM(square, jnp.float32),
            pltpu.SemaphoreType.DMA,
            pltpu.SemaphoreType.DMA((PANELS, row_count)),
            pltpu.SemaphoreType.DMA((PANELS,)),
            pltpu.SemaphoreType.DMA((PANELS, tiles_down, 3)),
            pltpu.SemaphoreType.DMA((PANELS, tiles_down)),
            pltpu.SemaphoreType.DMA((PANELS, tiles_across, row_count)),
            pltpu.SemaphoreType.DMA((PANELS, tiles_across)),
        ],
        compiler_params=pltpu.CompilerParams(
            collective_id=0, has_side_effects=True, vmem_limit_bytes=40 * 1024 * 1024
        ),
        name="panels",
    )(matrix)


def solution(mesh):
    return jax.shard_map(
        functools.partial(on_device, mesh.shape["row"], mesh.shape["col"]),
        mesh=mesh,
        in_specs=(P("row", "col"),),
        out_specs=P("row", "col"),
        check_vma=False,
    )
```

```python
import functools

import jax
import jax.numpy as jnp
from jax import lax
from jax.experimental import pallas as pl
from jax.experimental.pallas import tpu as pltpu
from jax.sharding import PartitionSpec as P

TILE = 256
PANELS = 3
SLAB = 64
GROUP = 8
LANES = 128
MESH = pl.DeviceIdType.MESH


def lane_splat(value, lane):
    return jnp.broadcast_to(value[:, lane : lane + 1], value.shape)


def row_splat(value, row):
    return jnp.broadcast_to(value[row : row + 1, :], value.shape)


def eliminate(tiles):
    finished = [[] for _ in tiles]
    for start in range(0, SLAB, GROUP):
        columns = [lane_splat(tiles[0], start + q) for q in range(GROUP)]
        row = lax.broadcasted_iota(jnp.int32, tiles[0].shape, 0)
        for j in range(0, GROUP, 2):
            c1, c2 = columns[j], columns[j + 1]
            a, b, d = row_splat(c1, j), row_splat(c1, j + 1), row_splat(c2, j + 1)
            ra = 1.0 / a
            rest = a / (a * d - b * b)
            ratio = b * ra
            m1 = jnp.where(row > j, c1 * ra, 0.0)
            m2 = jnp.where(row > j + 1, (c2 - c1 * ratio) * rest, 0.0)
            for q in range(j + 2, GROUP):
                x1 = row_splat(c1, q)
                x2 = row_splat(c2, q) - ratio * x1
                columns[q] = columns[q] - m1 * x1 - m2 * x2
            new = []
            for tile in tiles:
                r1 = row_splat(tile, j)
                r2 = row_splat(tile, j + 1) - ratio * r1
                new.append(tile - m1 * r1 - m2 * r2)
            tiles = new
        for kept, tile in zip(finished, tiles):
            kept.append(tile[:GROUP])
        tiles = [tile[GROUP:] for tile in tiles]
    tiles = [jnp.concatenate(kept, axis=0) for kept in finished]
    row = lax.broadcasted_iota(jnp.int32, tiles[0].shape, 0)
    lane = lax.broadcasted_iota(jnp.int32, tiles[0].shape, 1)
    pivots = jnp.sum(jnp.where(lane == row, tiles[0], 0.0), axis=1, keepdims=True)
    scale = lax.rsqrt(jnp.broadcast_to(pivots, tiles[0].shape))
    return [tile * scale for tile in tiles[1:]]


def precise_product(left, right):
    return jnp.dot(
        left,
        right,
        precision=lax.Precision.HIGHEST,
        preferred_element_type=jnp.float32,
    )


def factor_tile(square, inverse, upper):
    full = (TILE, TILE)
    eye = lax.broadcasted_iota(jnp.int32, full, 0) == lax.broadcasted_iota(jnp.int32, full, 1)
    inverse[...] = jnp.where(eye, 1.0, 0.0)
    upper[...] = jnp.zeros(full, jnp.float32)
    for first in range(0, TILE, SLAB):
        base = first // LANES * LANES
        reach = base + LANES
        shift = first - base
        rows = slice(first, first + SLAB)
        slab = [square[rows, s : s + LANES] for s in range(base, TILE, LANES)]
        back = [inverse[rows, s : s + LANES] for s in range(0, reach, LANES)]
        pivot = pltpu.roll(slab[0], LANES - shift, 1) if shift else slab[0]
        done = eliminate([pivot] + slab + back)
        top = jnp.concatenate(done[: len(slab)], axis=1) if len(slab) > 1 else done[0]
        low = done[len(slab) :]
        low = jnp.concatenate(low, axis=1) if len(low) > 1 else low[0]
        lane = lax.broadcasted_iota(jnp.int32, top.shape, 1)
        row = lax.broadcasted_iota(jnp.int32, top.shape, 0) + shift
        top = jnp.where(lane >= row, top, 0.0)
        upper[rows, base:] = top
        inverse[rows, :reach] = low
        flipped = top.T
        for near, far in ((first + SLAB, first + 2 * SLAB), (first + 2 * SLAB, TILE)):
            if near < far <= TILE:
                left = flipped[near - base : far - base]
                square[near:far, base:] -= precise_product(left, top)
                inverse[near:far, :reach] -= precise_product(left, low)


def kernel(
    row_count,
    col_count,
    matrix,
    out,
    block,
    rounded,
    across,
    inverses,
    square,
    upper,
    load_sem,
    inv_send,
    inv_recv,
    rows_send,
    rows_recv,
    across_send,
    across_recv,
):
    row, col = lax.axis_index("row"), lax.axis_index("col")
    tiles_down = block.shape[0] // TILE
    tiles_across = block.shape[1] // TILE
    load = pltpu.make_async_copy(matrix, block, load_sem)
    load.start()

    barrier = pltpu.get_barrier_semaphore()
    for step in range(1, row_count):
        other = lax.rem(row + step, row_count)
        pl.semaphore_signal(barrier, inc=1, device_id=(other, col), device_id_type=MESH)
    twin = col + 1 - 2 * lax.rem(col, 2)
    pl.semaphore_signal(barrier, inc=1, device_id=(row, twin), device_id_type=MESH)
    has_up = col + 2 < col_count
    has_down = col >= 2

    @pl.when(has_up)
    def _():
        pl.semaphore_signal(barrier, inc=1, device_id=(row, col + 2), device_id_type=MESH)

    @pl.when(has_down)
    def _():
        pl.semaphore_signal(barrier, inc=1, device_id=(row, col - 2), device_id_type=MESH)

    pl.semaphore_wait(barrier, row_count + has_up.astype(jnp.int32) + has_down.astype(jnp.int32))
    load.wait()

    def tile_rows(t):
        return pl.ds(pl.multiple_of(t * TILE, TILE), TILE)

    def inverse_copy(k, step):
        return pltpu.make_async_remote_copy(
            src_ref=inverses.at[k],
            dst_ref=inverses.at[k],
            send_sem=inv_send.at[k, step],
            recv_sem=inv_recv.at[k],
            device_id=(lax.rem(row + step, row_count), col),
            device_id_type=MESH,
        )

    def rows_copy(k, t, way, target):
        return pltpu.make_async_remote_copy(
            src_ref=rounded.at[k, t],
            dst_ref=rounded.at[k, t],
            send_sem=rows_send.at[k, t, way],
            recv_sem=rows_recv.at[k, t],
            device_id=(row, target),
            device_id_type=MESH,
        )

    def across_row(u):
        return (u * col_count + col) // row_count

    def across_copy(k, u, step):
        return pltpu.make_async_remote_copy(
            src_ref=rounded.at[k, across_row(u)],
            dst_ref=across.at[k, u],
            send_sem=across_send.at[k, u, step],
            recv_sem=across_recv.at[k, u],
            device_id=(lax.rem(row + step, row_count), col),
            device_id_type=MESH,
        )

    holds_across = row == lax.rem(col, row_count)

    def live(k, t):
        return t * row_count + row > k

    def sends(k, t):
        split = k == PANELS - 1
        odd = jnp.where(split, lax.rem(t, 2), 0)
        in_lane = lax.rem(col + k + odd, 2) == 0
        own_twin = k + 1 - 2 * lax.rem(k, 2)
        place, source = col // 2, k // 2
        up = jnp.logical_and(in_lane, jnp.logical_and(place >= source, has_up))
        down = jnp.logical_and(in_lane, jnp.logical_and(place <= source, has_down))
        returns = jnp.logical_and(split, jnp.logical_and(odd == 0, col == own_twin + 2))
        first = jnp.logical_and(col == k, jnp.logical_or(jnp.logical_not(split), odd == 1))
        cross = jnp.logical_or(first, jnp.logical_and(in_lane, place != source))
        ways = ((cross, twin), (up, col + 2), (jnp.logical_or(down, returns), col - 2))
        return tuple((jnp.logical_and(live(k, t), do), target) for do, target in ways)

    def arrival(k, step):
        own = lax.rem(col + k, 2)
        end = step == tiles_down - 1
        ahead = jnp.logical_or(step == 0, jnp.logical_and(lax.rem(step, 2) == 1, step < tiles_down - 1))
        place = jnp.where(
            ahead, (step + 1) // 2, jnp.where(end, tiles_down // 2 - 1, (step + tiles_down - 2) // 2 - tiles_down // 2)
        )
        mixed = 2 * place + jnp.where(ahead, own, 1 - own)
        return jnp.where(k == PANELS - 1, mixed, step)

    def pass_on(k, t):
        for way, (do, target) in enumerate(sends(k, t)):

            @pl.when(do)
            def _(way=way, target=target):
                rows_copy(k, t, way, target).start()

    def send_across(k, u):
        for step in range(1, row_count):
            across_copy(k, u, step).start()

    def update(k, u, t, partner):
        i, j = t * row_count + row, u * col_count + col

        @pl.when(jnp.logical_and(i >= j, j > k))
        def _():
            product = lax.dot_general(
                rounded[k, t],
                partner,
                (((1,), (1,)), ((), ())),
                preferred_element_type=jnp.float32,
            )
            block[tile_rows(t), u * TILE : (u + 1) * TILE] -= product

    def update_column(k, u, first):
        @pl.when(holds_across)
        def _():
            across[k, u] = rounded[k, across_row(u)]

        @pl.when(jnp.logical_not(holds_across))
        def _():
            across_copy(k, u, 1).wait_recv()

        def one(t, _):
            update(k, u, t, across[k, u])
            return 0

        lax.fori_loop(first, tiles_down, one, 0)

    def panel(k, _):
        last = k - 1
        ahead = jnp.logical_and(k < PANELS, jnp.logical_and(row == k, col == k))
        later = jnp.logical_and(ahead, k > 0)

        @pl.when(later)
        def _():
            rows_copy(last, 0, 0, twin).wait_recv()
            send_across(last, 0)
            update(last, 0, 0, rounded[last, 0])

        @pl.when(ahead)
        def _():
            square[...] = block[0:TILE, 0:TILE]
            factor_tile(square, inverses.at[k], upper)
            for step in range(1, row_count):
                inverse_copy(k, step).start()
            block[0:TILE, 0:TILE] = upper[...].T

        @pl.when(k > 0)
        def _():
            @pl.when(col != last)
            def _():
                def receive(step, _):
                    t = arrival(last, step)

                    @pl.when(live(last, t))
                    def _():
                        rows_copy(last, t, 0, twin).wait_recv()

                    @pl.when(jnp.logical_not(live(last, t)))
                    def _():
                        rounded[last, t] = jnp.zeros((TILE, TILE), jnp.bfloat16)

                    pass_on(last, t)
                    for u in range(tiles_across):

                        @pl.when(jnp.logical_and(holds_across, t == across_row(u)))
                        def _(u=u):
                            send_across(last, u)

                    return 0

                lax.fori_loop(later.astype(jnp.int32), tiles_down, receive, 0)

            @pl.when(jnp.logical_and(col == last, holds_across))
            def _():
                for u in range(tiles_across):
                    send_across(last, u)

            update_column(last, 0, later.astype(jnp.int32))

        @pl.when(jnp.logical_and(col == k, k < PANELS))
        def _():
            @pl.when(row != k)
            def _():
                inverse_copy(k, 1).wait_recv()

            def solve(t, _):
                below = t * row_count + row > k

                @pl.when(below)
                def _():
                    solved = lax.dot_general(
                        block[tile_rows(t), 0:TILE],
                        inverses[k],
                        (((1,), (1,)), ((), ())),
                        precision=lax.Precision.HIGHEST,
                        preferred_element_type=jnp.float32,
                    )
                    block[tile_rows(t), 0:TILE] = solved
                    rounded[k, t] = solved.astype(jnp.bfloat16)

                @pl.when(jnp.logical_not(below))
                def _():
                    rounded[k, t] = jnp.zeros((TILE, TILE), jnp.bfloat16)

                pass_on(k, t)
                return 0

            lax.fori_loop(0, tiles_down, solve, 0)

        @pl.when(k > 0)
        def _():
            for u in range(1, tiles_across):
                update_column(last, u, 0)

        return 0

    lax.fori_loop(0, PANELS + 1, panel, 0)

    store = pltpu.make_async_copy(block, out, load_sem)
    store.start()

    def finish(k, _):
        @pl.when(jnp.logical_and(row == k, col == k))
        def _():
            for step in range(1, row_count):
                inverse_copy(k, step).wait_send()

        def rows_done(t, _):
            for way, (do, target) in enumerate(sends(k, t)):

                @pl.when(do)
                def _(way=way, target=target):
                    rows_copy(k, t, way, target).wait_send()

            return 0

        lax.fori_loop(0, tiles_down, rows_done, 0)

        @pl.when(holds_across)
        def _():
            for u in range(tiles_across):
                for step in range(1, row_count):
                    across_copy(k, u, step).wait_send()

        return 0

    lax.fori_loop(0, PANELS, finish, 0)
    store.wait()


def on_device(row_count, col_count, matrix):
    tiles_down = matrix.shape[0] // TILE
    tiles_across = matrix.shape[1] // TILE
    square = (TILE, TILE)
    return pl.pallas_call(
        functools.partial(kernel, row_count, col_count),
        out_shape=jax.ShapeDtypeStruct(matrix.shape, jnp.float32),
        in_specs=[pl.BlockSpec(memory_space=pl.ANY)],
        out_specs=pl.BlockSpec(memory_space=pl.ANY),
        scratch_shapes=[
            pltpu.VMEM(matrix.shape, jnp.float32),
            pltpu.VMEM((PANELS, tiles_down) + square, jnp.bfloat16),
            pltpu.VMEM((PANELS, tiles_across) + square, jnp.bfloat16),
            pltpu.VMEM((PANELS,) + square, jnp.float32),
            pltpu.VMEM(square, jnp.float32),
            pltpu.VMEM(square, jnp.float32),
            pltpu.SemaphoreType.DMA,
            pltpu.SemaphoreType.DMA((PANELS, row_count)),
            pltpu.SemaphoreType.DMA((PANELS,)),
            pltpu.SemaphoreType.DMA((PANELS, tiles_down, 3)),
            pltpu.SemaphoreType.DMA((PANELS, tiles_down)),
            pltpu.SemaphoreType.DMA((PANELS, tiles_across, row_count)),
            pltpu.SemaphoreType.DMA((PANELS, tiles_across)),
        ],
        compiler_params=pltpu.CompilerParams(
            collective_id=0, has_side_effects=True, vmem_limit_bytes=40 * 1024 * 1024
        ),
        name="panels",
    )(matrix)


def solution(mesh):
    return jax.shard_map(
        functools.partial(on_device, mesh.shape["row"], mesh.shape["col"]),
        mesh=mesh,
        in_specs=(P("row", "col"),),
        out_specs=P("row", "col"),
        check_vma=False,
    )
```

```python
import functools

import jax
import jax.numpy as jnp
from jax import lax
from jax.experimental import pallas as pl
from jax.experimental.pallas import tpu as pltpu
from jax.sharding import PartitionSpec as P

TILE = 256
PANELS = 3
SLAB = 64
GROUP = 16
LANES = 128
MESH = pl.DeviceIdType.MESH


def lane_splat(value, lane):
    return jnp.broadcast_to(value[:, lane : lane + 1], value.shape)


def row_splat(value, row):
    return jnp.broadcast_to(value[row : row + 1, :], value.shape)


def eliminate(tiles):
    finished = [[] for _ in tiles]
    for start in range(0, SLAB, GROUP):
        columns = [lane_splat(tiles[0], start + q) for q in range(GROUP)]
        row = lax.broadcasted_iota(jnp.int32, tiles[0].shape, 0)
        for j in range(0, GROUP, 2):
            c1, c2 = columns[j], columns[j + 1]
            a, b, d = row_splat(c1, j), row_splat(c1, j + 1), row_splat(c2, j + 1)
            ra = 1.0 / a
            rest = a / (a * d - b * b)
            ratio = b * ra
            m1 = jnp.where(row > j, c1 * ra, 0.0)
            m2 = jnp.where(row > j + 1, (c2 - c1 * ratio) * rest, 0.0)
            for q in range(j + 2, GROUP):
                x1 = row_splat(c1, q)
                x2 = row_splat(c2, q) - ratio * x1
                columns[q] = columns[q] - m1 * x1 - m2 * x2
            new = []
            for tile in tiles:
                r1 = row_splat(tile, j)
                r2 = row_splat(tile, j + 1) - ratio * r1
                new.append(tile - m1 * r1 - m2 * r2)
            tiles = new
        for kept, tile in zip(finished, tiles):
            kept.append(tile[:GROUP])
        tiles = [tile[GROUP:] for tile in tiles]
    tiles = [jnp.concatenate(kept, axis=0) for kept in finished]
    row = lax.broadcasted_iota(jnp.int32, tiles[0].shape, 0)
    lane = lax.broadcasted_iota(jnp.int32, tiles[0].shape, 1)
    pivots = jnp.sum(jnp.where(lane == row, tiles[0], 0.0), axis=1, keepdims=True)
    scale = lax.rsqrt(jnp.broadcast_to(pivots, tiles[0].shape))
    return [tile * scale for tile in tiles[1:]]


def precise_product(left, right):
    return jnp.dot(
        left,
        right,
        precision=lax.Precision.HIGHEST,
        preferred_element_type=jnp.float32,
    )


def factor_tile(square, inverse, upper):
    full = (TILE, TILE)
    eye = lax.broadcasted_iota(jnp.int32, full, 0) == lax.broadcasted_iota(jnp.int32, full, 1)
    inverse[...] = jnp.where(eye, 1.0, 0.0)
    upper[...] = jnp.zeros(full, jnp.float32)
    for first in range(0, TILE, SLAB):
        base = first // LANES * LANES
        reach = base + LANES
        shift = first - base
        rows = slice(first, first + SLAB)
        slab = [square[rows, s : s + LANES] for s in range(base, TILE, LANES)]
        back = [inverse[rows, s : s + LANES] for s in range(0, reach, LANES)]
        pivot = pltpu.roll(slab[0], LANES - shift, 1) if shift else slab[0]
        done = eliminate([pivot] + slab + back)
        top = jnp.concatenate(done[: len(slab)], axis=1) if len(slab) > 1 else done[0]
        low = done[len(slab) :]
        low = jnp.concatenate(low, axis=1) if len(low) > 1 else low[0]
        lane = lax.broadcasted_iota(jnp.int32, top.shape, 1)
        row = lax.broadcasted_iota(jnp.int32, top.shape, 0) + shift
        top = jnp.where(lane >= row, top, 0.0)
        upper[rows, base:] = top
        inverse[rows, :reach] = low
        flipped = top.T
        for near, far in ((first + SLAB, first + 2 * SLAB), (first + 2 * SLAB, TILE)):
            if near < far <= TILE:
                left = flipped[near - base : far - base]
                square[near:far, base:] -= precise_product(left, top)
                inverse[near:far, :reach] -= precise_product(left, low)


def kernel(
    row_count,
    col_count,
    matrix,
    out,
    block,
    rounded,
    across,
    inverses,
    square,
    upper,
    load_sem,
    inv_send,
    inv_recv,
    rows_send,
    rows_recv,
    across_send,
    across_recv,
):
    row, col = lax.axis_index("row"), lax.axis_index("col")
    tiles_down = block.shape[0] // TILE
    tiles_across = block.shape[1] // TILE
    load = pltpu.make_async_copy(matrix, block, load_sem)
    load.start()

    barrier = pltpu.get_barrier_semaphore()
    for step in range(1, row_count):
        other = lax.rem(row + step, row_count)
        pl.semaphore_signal(barrier, inc=1, device_id=(other, col), device_id_type=MESH)
    twin = col + 1 - 2 * lax.rem(col, 2)
    pl.semaphore_signal(barrier, inc=1, device_id=(row, twin), device_id_type=MESH)
    has_up = col + 2 < col_count
    has_down = col >= 2

    @pl.when(has_up)
    def _():
        pl.semaphore_signal(barrier, inc=1, device_id=(row, col + 2), device_id_type=MESH)

    @pl.when(has_down)
    def _():
        pl.semaphore_signal(barrier, inc=1, device_id=(row, col - 2), device_id_type=MESH)

    pl.semaphore_wait(barrier, row_count + has_up.astype(jnp.int32) + has_down.astype(jnp.int32))
    load.wait()

    def tile_rows(t):
        return pl.ds(pl.multiple_of(t * TILE, TILE), TILE)

    def inverse_copy(k, step):
        return pltpu.make_async_remote_copy(
            src_ref=inverses.at[k],
            dst_ref=inverses.at[k],
            send_sem=inv_send.at[k, step],
            recv_sem=inv_recv.at[k],
            device_id=(lax.rem(row + step, row_count), col),
            device_id_type=MESH,
        )

    def rows_copy(k, t, way, target):
        return pltpu.make_async_remote_copy(
            src_ref=rounded.at[k, t],
            dst_ref=rounded.at[k, t],
            send_sem=rows_send.at[k, t, way],
            recv_sem=rows_recv.at[k, t],
            device_id=(row, target),
            device_id_type=MESH,
        )

    def across_row(u):
        return (u * col_count + col) // row_count

    def across_copy(k, u, step):
        return pltpu.make_async_remote_copy(
            src_ref=rounded.at[k, across_row(u)],
            dst_ref=across.at[k, u],
            send_sem=across_send.at[k, u, step],
            recv_sem=across_recv.at[k, u],
            device_id=(lax.rem(row + step, row_count), col),
            device_id_type=MESH,
        )

    holds_across = row == lax.rem(col, row_count)

    def live(k, t):
        return t * row_count + row > k

    def sends(k, t):
        split = k == PANELS - 1
        odd = jnp.where(split, lax.rem(t, 2), 0)
        in_lane = lax.rem(col + k + odd, 2) == 0
        own_twin = k + 1 - 2 * lax.rem(k, 2)
        place, source = col // 2, k // 2
        up = jnp.logical_and(in_lane, jnp.logical_and(place >= source, has_up))
        down = jnp.logical_and(in_lane, jnp.logical_and(place <= source, has_down))
        returns = jnp.logical_and(split, jnp.logical_and(odd == 0, col == own_twin + 2))
        first = jnp.logical_and(col == k, jnp.logical_or(jnp.logical_not(split), odd == 1))
        cross = jnp.logical_or(first, jnp.logical_and(in_lane, place != source))
        ways = ((cross, twin), (up, col + 2), (jnp.logical_or(down, returns), col - 2))
        return tuple((jnp.logical_and(live(k, t), do), target) for do, target in ways)

    def arrival(k, step):
        own = lax.rem(col + k, 2)
        end = step == tiles_down - 1
        ahead = jnp.logical_or(step == 0, jnp.logical_and(lax.rem(step, 2) == 1, step < tiles_down - 1))
        place = jnp.where(
            ahead, (step + 1) // 2, jnp.where(end, tiles_down // 2 - 1, (step + tiles_down - 2) // 2 - tiles_down // 2)
        )
        mixed = 2 * place + jnp.where(ahead, own, 1 - own)
        return jnp.where(k == PANELS - 1, mixed, step)

    def pass_on(k, t):
        for way, (do, target) in enumerate(sends(k, t)):

            @pl.when(do)
            def _(way=way, target=target):
                rows_copy(k, t, way, target).start()

    def send_across(k, u):
        for step in range(1, row_count):
            across_copy(k, u, step).start()

    def update(k, u, t, partner):
        i, j = t * row_count + row, u * col_count + col

        @pl.when(jnp.logical_and(i >= j, j > k))
        def _():
            product = lax.dot_general(
                rounded[k, t],
                partner,
                (((1,), (1,)), ((), ())),
                preferred_element_type=jnp.float32,
            )
            block[tile_rows(t), u * TILE : (u + 1) * TILE] -= product

    def update_column(k, u, first):
        @pl.when(holds_across)
        def _():
            across[k, u] = rounded[k, across_row(u)]

        @pl.when(jnp.logical_not(holds_across))
        def _():
            across_copy(k, u, 1).wait_recv()

        def one(t, _):
            update(k, u, t, across[k, u])
            return 0

        lax.fori_loop(first, tiles_down, one, 0)

    def panel(k, _):
        last = k - 1
        ahead = jnp.logical_and(k < PANELS, jnp.logical_and(row == k, col == k))
        later = jnp.logical_and(ahead, k > 0)

        @pl.when(later)
        def _():
            rows_copy(last, 0, 0, twin).wait_recv()
            send_across(last, 0)
            update(last, 0, 0, rounded[last, 0])

        @pl.when(ahead)
        def _():
            square[...] = block[0:TILE, 0:TILE]
            factor_tile(square, inverses.at[k], upper)
            for step in range(1, row_count):
                inverse_copy(k, step).start()
            block[0:TILE, 0:TILE] = upper[...].T

        @pl.when(k > 0)
        def _():
            @pl.when(col != last)
            def _():
                def receive(step, _):
                    t = arrival(last, step)

                    @pl.when(live(last, t))
                    def _():
                        rows_copy(last, t, 0, twin).wait_recv()

                    @pl.when(jnp.logical_not(live(last, t)))
                    def _():
                        rounded[last, t] = jnp.zeros((TILE, TILE), jnp.bfloat16)

                    pass_on(last, t)
                    for u in range(tiles_across):

                        @pl.when(jnp.logical_and(holds_across, t == across_row(u)))
                        def _(u=u):
                            send_across(last, u)

                    return 0

                lax.fori_loop(later.astype(jnp.int32), tiles_down, receive, 0)

            @pl.when(jnp.logical_and(col == last, holds_across))
            def _():
                for u in range(tiles_across):
                    send_across(last, u)

            update_column(last, 0, later.astype(jnp.int32))

        @pl.when(jnp.logical_and(col == k, k < PANELS))
        def _():
            @pl.when(row != k)
            def _():
                inverse_copy(k, 1).wait_recv()

            def solve(t, _):
                below = t * row_count + row > k

                @pl.when(below)
                def _():
                    solved = lax.dot_general(
                        block[tile_rows(t), 0:TILE],
                        inverses[k],
                        (((1,), (1,)), ((), ())),
                        precision=lax.Precision.HIGHEST,
                        preferred_element_type=jnp.float32,
                    )
                    block[tile_rows(t), 0:TILE] = solved
                    rounded[k, t] = solved.astype(jnp.bfloat16)

                @pl.when(jnp.logical_not(below))
                def _():
                    rounded[k, t] = jnp.zeros((TILE, TILE), jnp.bfloat16)

                pass_on(k, t)
                return 0

            lax.fori_loop(0, tiles_down, solve, 0)

        @pl.when(k > 0)
        def _():
            for u in range(1, tiles_across):
                update_column(last, u, 0)

        return 0

    lax.fori_loop(0, PANELS + 1, panel, 0)

    store = pltpu.make_async_copy(block, out, load_sem)
    store.start()

    def finish(k, _):
        @pl.when(jnp.logical_and(row == k, col == k))
        def _():
            for step in range(1, row_count):
                inverse_copy(k, step).wait_send()

        def rows_done(t, _):
            for way, (do, target) in enumerate(sends(k, t)):

                @pl.when(do)
                def _(way=way, target=target):
                    rows_copy(k, t, way, target).wait_send()

            return 0

        lax.fori_loop(0, tiles_down, rows_done, 0)

        @pl.when(holds_across)
        def _():
            for u in range(tiles_across):
                for step in range(1, row_count):
                    across_copy(k, u, step).wait_send()

        return 0

    lax.fori_loop(0, PANELS, finish, 0)
    store.wait()


def on_device(row_count, col_count, matrix):
    tiles_down = matrix.shape[0] // TILE
    tiles_across = matrix.shape[1] // TILE
    square = (TILE, TILE)
    return pl.pallas_call(
        functools.partial(kernel, row_count, col_count),
        out_shape=jax.ShapeDtypeStruct(matrix.shape, jnp.float32),
        in_specs=[pl.BlockSpec(memory_space=pl.ANY)],
        out_specs=pl.BlockSpec(memory_space=pl.ANY),
        scratch_shapes=[
            pltpu.VMEM(matrix.shape, jnp.float32),
            pltpu.VMEM((PANELS, tiles_down) + square, jnp.bfloat16),
            pltpu.VMEM((PANELS, tiles_across) + square, jnp.bfloat16),
            pltpu.VMEM((PANELS,) + square, jnp.float32),
            pltpu.VMEM(square, jnp.float32),
            pltpu.VMEM(square, jnp.float32),
            pltpu.SemaphoreType.DMA,
            pltpu.SemaphoreType.DMA((PANELS, row_count)),
            pltpu.SemaphoreType.DMA((PANELS,)),
            pltpu.SemaphoreType.DMA((PANELS, tiles_down, 3)),
            pltpu.SemaphoreType.DMA((PANELS, tiles_down)),
            pltpu.SemaphoreType.DMA((PANELS, tiles_across, row_count)),
            pltpu.SemaphoreType.DMA((PANELS, tiles_across)),
        ],
        compiler_params=pltpu.CompilerParams(
            collective_id=0, has_side_effects=True, vmem_limit_bytes=40 * 1024 * 1024
        ),
        name="panels",
    )(matrix)


def solution(mesh):
    return jax.shard_map(
        functools.partial(on_device, mesh.shape["row"], mesh.shape["col"]),
        mesh=mesh,
        in_specs=(P("row", "col"),),
        out_specs=P("row", "col"),
        check_vma=False,
    )
```
